32 devices in a mesh: dev: 32 (over z, y, x, core).
Axes of the slice: x: 2, y: 2, z: 4, core: 2. Of those that a mesh axis runs over, the one named last changes fastest.
Arguments:
- diagonal: float32 [16384, 512], P('dev'), may hold values from -50 to 250, as said below
- panel: bfloat16 [98304, 512], P('dev'), may hold values from -3 to 3
- counts: int32 [32], P('dev'), may hold values from 1 to 6, 112 in all
- target_map: int32 [32, 21], P('dev'), may hold values from 0 to 7
- trailing: float32 [16384, 512], P('dev'), may hold values from -6 to 6
Outputs:
- diag_factor: float32 [16384, 512], P('dev')
- panel_factor: bfloat16 [98304, 512], P('dev')
- updated: float32 [16384, 512], P('dev')
- logdet_mean: float32 [], replicated
The draws below stay inside these ranges and needn't reach their ends.
Inputs may be any that keep to these rules, and one draw needn't show every extreme that they name: Each block of 512 rows of diagonal is symmetric positive definite. `counts`: some supernode holds 6 panel blocks.
All inputs are finite; a program needn't handle non-finite values.
Results may differ from the reference program's by a relative error of at most 0.006.
Values may be sent and summed in bfloat16 or wider, within the bound.
A program may use at most 128 MiB of HBM per device.

```python
import math
import jax
import jax.numpy as jnp
import numpy as np
from jax import lax

W = 512
PB = 6
GROUP = 8
SUP = 32
PAIRS = 21
N_DEV = 32


def draw_diagonal(key, part):
    first, second = jax.random.split(jax.random.fold_in(key, 7))
    noise = jax.random.normal(first, (N_DEV, W, W), jnp.float32)
    gram = jnp.einsum('sik,sjk->sij', noise, noise) / W
    spread = jax.random.uniform(second, (N_DEV,), jnp.float32, 0.8, 1.25)
    level = jnp.exp(0.5 + 3.0 * jnp.arange(N_DEV, dtype=jnp.float32) / (N_DEV - 1))
    blocks = (level * spread)[:, None, None] * (gram + 2.0 * jnp.eye(W, dtype=jnp.float32)[None])
    return blocks.reshape(N_DEV * W, W)


def set_ends(result, own_key, smallest, top_value):
    place = [jax.random.randint(jax.random.fold_in(own_key, axis), (), 0, length) for axis, length in enumerate(result.shape)]
    main_axis = result.shape.index(max(result.shape))
    neighbour = place[:main_axis] + [(place[main_axis] + 1) % result.shape[main_axis]] + place[main_axis + 1:]
    return result.at[tuple(place)].set(smallest).at[tuple(neighbour)].set(top_value)


def levels(own_key, shape, cuts, smallest, largest):
    factor_of = 1.0
    for dim, blocks in cuts:
        steps = jax.random.uniform(jax.random.fold_in(jax.random.fold_in(own_key, 6), dim), (blocks,), jnp.float32, smallest / len(cuts), largest / len(cuts))
        factor_of = factor_of * jnp.repeat(jnp.exp(steps), shape[dim] // blocks).reshape((-1,) + (1,) * (len(shape) - 1 - dim))
    return factor_of


def split_up(amount, total, reach, skew):
    loads = [(1 << 20) // math.isqrt(standing ** skew) + 1 for standing in range(2, amount + 1)]
    surplus, given = total - reach - (amount - 1), [1] * (amount - 1)
    while surplus > 0:
        candidates = [i for i in range(amount - 1) if given[i] < reach]
        mass, left = sum([loads[i] for i in candidates]), surplus
        for i in candidates:
            extra = min(reach - given[i], max(1, left * loads[i] // mass), surplus)
            given[i] = given[i] + extra
            surplus = surplus - extra
    return np.array([reach] + given)


def ragged_sizes(key, count, total, bound, skew):
    if count == 2:
        one = jax.random.randint(key, (), max(1, total - bound), min(bound, total - 1) + 1)
        return jnp.stack([one, total - one])
    tallies = jnp.asarray(split_up(count, total, bound, skew), jnp.int32)
    twos = (count - 1) // 2
    donor, sink = tallies[1:1 + 2 * twos:2], tallies[2:2 + 2 * twos:2]
    slack = jnp.minimum(donor - 1, bound - sink)
    shifted = jax.random.randint(jax.random.fold_in(key, 1), (twos,), 0, 1 << 20) % (slack + 1)
    tallies = tallies.at[1:1 + 2 * twos:2].set(donor - shifted).at[2:2 + 2 * twos:2].set(sink + shifted)
    return tallies[jax.random.permutation(jax.random.fold_in(key, 2), count)]


def gaussian(key, dims, scale, bound, cuts=(), kind=jnp.bfloat16):
    entries = scale * jax.random.normal(key, dims, jnp.float32)
    if cuts:
        entries = entries * levels(key, dims, cuts, -0.22, 0.18)
    return jnp.clip(entries, -bound, bound).astype(kind)


def setup_inputs(seed: int = 0) -> dict:
    keys = jax.random.split(jax.random.key(seed), 6)
    return {
        "diagonal": draw_diagonal(jax.random.fold_in(keys[5], 71), 0),
        "panel": gaussian(keys[1], (SUP * PB * W, W), 0.5, 3.0, ((0, 32),)),
        "counts": ragged_sizes(keys[2], SUP, SUP * (PB + 1) // 2, PB, 0).astype(jnp.int32),
        "target_map": set_ends(jax.random.randint(keys[3], (SUP, PAIRS), 0, GROUP), jax.random.fold_in(keys[3], 1), 0, GROUP - 1).astype(jnp.int32),
        "trailing": gaussian(keys[4], (SUP * W, W), 1.0, 6.0, ((0, 32),), jnp.float32),
    }


def pair_tables(block_count):
    pair_rows = [i for i in range(block_count) for j in range(i + 1)]
    pair_cols = [j for i in range(block_count) for j in range(i + 1)]
    return (pair_rows, pair_cols)

def factor_one(diag_block, panel_block, block_count):
    factor = jnp.linalg.cholesky(diag_block)
    solved = lax.linalg.triangular_solve(factor, panel_block.astype(jnp.float32), left_side=False, lower=True, transpose_a=True)
    block_of_row = jnp.arange(PB * W, dtype=jnp.int32) // W
    solved = jnp.where((block_of_row < block_count)[:, None], solved, jnp.zeros_like(solved)).astype(jnp.bfloat16)
    logterm = 2.0 * jnp.sum(jnp.log(jnp.diagonal(factor)))
    return (factor, solved, logterm)

def reference(diagonal, panel, counts, target_map, trailing):
    diag_blocks = diagonal.reshape(N_DEV, W, W)
    panel_blocks = panel.reshape(N_DEV, PB * W, W)
    totals = trailing.reshape(N_DEV, W, W)
    pair_rows, pair_cols = pair_tables(PB)

    def eliminate(running, inputs):
        totals, logsum = running
        node_index, diag_block, panel_block, block_count, targets = inputs
        factor, solved, logterm = factor_one(diag_block, panel_block, block_count)
        base = node_index // GROUP * GROUP
        for pair_index in range(len(pair_rows)):
            left_block = solved[pair_rows[pair_index] * W:(pair_rows[pair_index] + 1) * W]
            right_block = solved[pair_cols[pair_index] * W:(pair_cols[pair_index] + 1) * W]
            update = lax.dot_general(left_block.astype(jnp.float32), right_block.astype(jnp.float32), (((1,), (1,)), ((), ())), preferred_element_type=jnp.float32)
            target_row = (base + targets[pair_index]).astype(jnp.int32)
            totals = totals.at[target_row].add(-update)
        return ((totals, logsum + logterm), (factor, solved))
    inputs = (jnp.arange(N_DEV, dtype=jnp.int32), diag_blocks, panel_blocks, counts, target_map)
    (totals, logsum), (factors, solved) = lax.scan(eliminate, (totals, jnp.zeros((), jnp.float32)), inputs)
    return (factors.reshape(N_DEV * W, W), solved.reshape(N_DEV * PB * W, W), totals.reshape(N_DEV * W, W), logsum / (N_DEV * W))
```

```python
import functools

import jax
import jax.numpy as jnp
from jax import lax
from jax.experimental import pallas as pl
from jax.experimental.pallas import tpu as pltpu
from jax.sharding import PartitionSpec as P

GROUP = 8
BASE = 128
STEP = 8
ROWS = 8


def dot_t(left, right, precision=None):
    return lax.dot_general(
        left, right, (((1,), (1,)), ((), ())), precision=precision, preferred_element_type=jnp.float32
    )


def factor_base(block):
    size = block.shape[0]
    shape = (ROWS, size)
    groups = size // ROWS
    sublane = lax.broadcasted_iota(jnp.int32, shape, 0)
    lane = lax.broadcasted_iota(jnp.int32, shape, 1)
    work = [block[g * ROWS : (g + 1) * ROWS, :] for g in range(groups)]
    side = [jnp.where(lane == sublane + g * ROWS, 1.0, 0.0).astype(jnp.float32) for g in range(groups)]
    upper, inverse = [None] * groups, [None] * groups
    for first in range(0, size, STEP):
        own, offset = first // ROWS, first % ROWS
        following = range((first + STEP) // ROWS, groups)
        columns = {
            g: [jnp.broadcast_to(work[g][:, first + j : first + j + 1], shape) for j in range(STEP)]
            for g in sorted({own, *following})
        }
        entry = {
            (i, j): jnp.broadcast_to(columns[own][j][offset + i : offset + i + 1, :], shape)
            for j in range(STEP)
            for i in range(j, STEP)
        }
        scale = []
        for j in range(STEP):
            scale.append(lax.rsqrt(entry[j, j]))
            for i in range(j + 1, STEP):
                entry[i, j] = entry[i, j] * scale[j]
            for i in range(j + 1, STEP):
                for m in range(j + 1, i + 1):
                    entry[i, m] = entry[i, m] - entry[i, j] * entry[m, j]
        rows, side_rows = [], []
        for j in range(STEP):
            row = jnp.broadcast_to(work[own][offset + j : offset + j + 1, :], shape)
            side_row = jnp.broadcast_to(side[own][offset + j : offset + j + 1, :], shape)
            for m in range(j):
                row = row - entry[j, m] * rows[m]
                side_row = side_row - entry[j, m] * side_rows[m]
            rows.append(row * scale[j])
            side_rows.append(side_row * scale[j])
        for j in range(STEP):
            at = sublane == offset + j
            upper[own] = rows[j] if upper[own] is None else jnp.where(at, rows[j], upper[own])
            inverse[own] = side_rows[j] if inverse[own] is None else jnp.where(at, side_rows[j], inverse[own])
        for g in following:
            lower = []
            for j in range(STEP):
                column = columns[g][j]
                for m in range(j):
                    column = column - lower[m] * entry[j, m]
                lower.append(column * scale[j])
            for j in range(STEP):
                work[g] = work[g] - lower[j] * rows[j]
                side[g] = side[g] - lower[j] * side_rows[j]
    return jnp.concatenate(upper, axis=0), jnp.concatenate(inverse, axis=0)


def factor_kernel(
    counts, targets, diagonal, panel, factor, solved, sums, logterm, work, inverse, high, low, totals
):
    width = diagonal.shape[0]
    blocks = panel.shape[0] // width
    steps = width // BASE
    exact = lax.Precision.HIGHEST
    work[...] = diagonal[...]
    factor[...] = jnp.zeros_like(factor)
    inverse[...] = jnp.zeros_like(inverse)
    totals[...] = jnp.zeros_like(totals)
    row = lax.broadcasted_iota(jnp.int32, (BASE, BASE), 0)
    col = lax.broadcasted_iota(jnp.int32, (BASE, BASE), 1)

    def eliminate(step, logs):
        here = pl.ds(pl.multiple_of(step * BASE, BASE), BASE)
        upper, inverted = factor_base(work[here, here])
        factor[here, here] = jnp.where(row >= col, upper.T, 0.0)
        inverse[here, here] = inverted
        for static in range(steps):

            @pl.when(step == static)
            def _():
                start, stop = static * BASE, (static + 1) * BASE
                own = inverse[start:stop, start:stop]
                if stop < width:
                    below = dot_t(work[stop:, start:stop], own, exact)
                    factor[stop:, start:stop] = below
                    work[stop:, stop:] -= dot_t(below, below, exact)
                if start > 0:
                    product = jnp.dot(
                        factor[start:stop, :start],
                        inverse[:start, :start],
                        precision=exact,
                        preferred_element_type=jnp.float32,
                    )
                    inverse[start:stop, :start] = -jnp.dot(
                        own, product, precision=exact, preferred_element_type=jnp.float32
                    )

        pivots = jnp.sum(jnp.where(row == col, upper, 0.0), axis=0, keepdims=True)
        return logs + jnp.log(pivots)

    logs = lax.fori_loop(0, steps, eliminate, jnp.zeros((1, BASE), jnp.float32))
    logterm[...] = jnp.broadcast_to(2.0 * jnp.sum(logs, axis=1, keepdims=True), logterm.shape)
    high[...] = inverse[...].astype(jnp.bfloat16)
    low[...] = (inverse[...] - high[...].astype(jnp.float32)).astype(jnp.bfloat16)
    live = counts[0]
    half = width // 2

    def solve(block, _):
        here = pl.ds(pl.multiple_of(block * width, width), width)

        @pl.when(block < live)
        def _():
            left = panel[here, :half]
            solved[here, :half] = (
                dot_t(left, high[:half, :half]) + dot_t(left, low[:half, :half])
            ).astype(jnp.bfloat16)
            left = panel[here, :]
            solved[here, half:] = (dot_t(left, high[half:, :]) + dot_t(left, low[half:, :])).astype(jnp.bfloat16)

        @pl.when(block >= live)
        def _():
            solved[here, :] = jnp.zeros((width, width), jnp.bfloat16)

        return 0

    lax.fori_loop(0, blocks, solve, 0)

    def update_row(i, _):
        left = pl.ds(pl.multiple_of(i * width, width), width)

        def update(j, _):
            right = pl.ds(pl.multiple_of(j * width, width), width)
            target = targets[0, i * (i + 1) // 2 + j]
            totals[target] += dot_t(solved[left, :], solved[right, :])
            return 0

        return lax.fori_loop(0, i + 1, update, 0)

    lax.fori_loop(0, live, update_row, 0)
    for target in range(GROUP):
        sums[target] = (-totals[target]).astype(sums.dtype)


def factor_and_update(diagonal, panel, counts, target_map):
    width = diagonal.shape[1]
    vmem = pl.BlockSpec(memory_space=pltpu.VMEM)
    smem = pl.BlockSpec(memory_space=pltpu.SMEM)
    return pl.pallas_call(
        factor_kernel,
        out_shape=(
            jax.ShapeDtypeStruct(diagonal.shape, jnp.float32),
            jax.ShapeDtypeStruct(panel.shape, jnp.bfloat16),
            jax.ShapeDtypeStruct((GROUP, width, width), jnp.bfloat16),
            jax.ShapeDtypeStruct((8, 128), jnp.float32),
        ),
        in_specs=[smem, smem, vmem, vmem],
        out_specs=(vmem, vmem, vmem, vmem),
        scratch_shapes=[
            pltpu.VMEM((width, width), jnp.float32),
            pltpu.VMEM((width, width), jnp.float32),
            pltpu.VMEM((width, width), jnp.bfloat16),
            pltpu.VMEM((width, width), jnp.bfloat16),
            pltpu.VMEM((GROUP, width, width), jnp.float32),
        ],
        compiler_params=pltpu.CompilerParams(vmem_limit_bytes=48 * 1024 * 1024),
        name="factor_and_update",
    )(counts, target_map, diagonal, panel)


def from_partner(block, axis, distance):
    count = lax.axis_size(axis)
    route = []
    for low in range(count):
        high = low | 1 << distance
        if high != low and high < count:
            route += [(low, high), (high, low)]
    return lax.ppermute(block, axis, route)


def local(diagonal, panel, counts, target_map, trailing):
    block_width = diagonal.shape[1]
    factor, panel_factor, totals, logterm = factor_and_update(diagonal, panel, counts, target_map)
    logdet_total = lax.psum(logterm[0, 0], "dev")
    logdet_mean = logdet_total / (lax.axis_size("dev") * block_width)
    member = lax.axis_index("dev") % GROUP
    half_size = GROUP
    totals = totals.reshape((2,) * (GROUP.bit_length() - 1) + totals.shape[1:])
    for bit_number in range(GROUP.bit_length() - 1):
        axis = totals.ndim - 3
        upper_bit = member // 2**bit_number % 2
        kept_half = lax.dynamic_index_in_dim(totals, upper_bit, axis, keepdims=False)
        sent_half = lax.dynamic_index_in_dim(totals, 1 - upper_bit, axis, keepdims=False)
        totals = kept_half.astype(jnp.float32) + from_partner(
            sent_half.astype(jnp.bfloat16), "dev", bit_number
        ).astype(jnp.float32)
    updated = trailing + totals
    return (factor, panel_factor, updated, logdet_mean)


def solution(mesh):
    return jax.shard_map(
        local,
        mesh=mesh,
        in_specs=(P("dev", None), P("dev", None), P("dev"), P("dev", None), P("dev", None)),
        out_specs=(P("dev", None), P("dev", None), P("dev", None), P()),
        check_vma=False,
    )
```

```python
import functools

import jax
import jax.numpy as jnp
from jax import lax
from jax.experimental import pallas as pl
from jax.experimental.pallas import tpu as pltpu
from jax.sharding import PartitionSpec as P

GROUP = 8
BASE = 128
STEP = 8
ROWS = 8


def dot_t(left, right, precision=None):
    return lax.dot_general(
        left, right, (((1,), (1,)), ((), ())), precision=precision, preferred_element_type=jnp.float32
    )


def factor_base(block):
    size = block.shape[0]
    shape = (ROWS, size)
    groups = size // ROWS
    sublane = lax.broadcasted_iota(jnp.int32, shape, 0)
    lane = lax.broadcasted_iota(jnp.int32, shape, 1)
    work = [block[g * ROWS : (g + 1) * ROWS, :] for g in range(groups)]
    side = [jnp.where(lane == sublane + g * ROWS, 1.0, 0.0).astype(jnp.float32) for g in range(groups)]
    upper, inverse = [None] * groups, [None] * groups
    for first in range(0, size, STEP):
        own, offset = first // ROWS, first % ROWS
        following = range((first + STEP) // ROWS, groups)
        columns = {
            g: [jnp.broadcast_to(work[g][:, first + j : first + j + 1], shape) for j in range(STEP)]
            for g in sorted({own, *following})
        }
        entry = {
            (i, j): jnp.broadcast_to(columns[own][j][offset + i : offset + i + 1, :], shape)
            for j in range(STEP)
            for i in range(j, STEP)
        }
        scale = []
        for j in range(STEP):
            scale.append(lax.rsqrt(entry[j, j]))
            for i in range(j + 1, STEP):
                entry[i, j] = entry[i, j] * scale[j]
            for i in range(j + 1, STEP):
                for m in range(j + 1, i + 1):
                    entry[i, m] = entry[i, m] - entry[i, j] * entry[m, j]
        rows, side_rows = [], []
        for j in range(STEP):
            row = jnp.broadcast_to(work[own][offset + j : offset + j + 1, :], shape)
            side_row = jnp.broadcast_to(side[own][offset + j : offset + j + 1, :], shape)
            for m in range(j):
                row = row - entry[j, m] * rows[m]
                side_row = side_row - entry[j, m] * side_rows[m]
            rows.append(row * scale[j])
            side_rows.append(side_row * scale[j])
        for j in range(STEP):
            at = sublane == offset + j
            upper[own] = rows[j] if upper[own] is None else jnp.where(at, rows[j], upper[own])
            inverse[own] = side_rows[j] if inverse[own] is None else jnp.where(at, side_rows[j], inverse[own])
        for g in following:
            lower = []
            for j in range(STEP):
                column = columns[g][j]
                for m in range(j):
                    column = column - lower[m] * entry[j, m]
                lower.append(column * scale[j])
            for j in range(STEP):
                work[g] = work[g] - lower[j] * rows[j]
                side[g] = side[g] - lower[j] * side_rows[j]
    return jnp.concatenate(upper, axis=0), jnp.concatenate(inverse, axis=0)


def factor_kernel(
    counts,
    targets,
    diagonal,
    panel_source,
    factor_result,
    solved_result,
    sums_result,
    logterm,
    work,
    inverse,
    high,
    low,
    totals,
    factor,
    panel,
    solved,
    panel_sem,
    factor_sem,
    solved_sem,
    sums,
    sums_sem,
):
    width = diagonal.shape[0]
    blocks = panel.shape[0] // width
    fetch = pltpu.make_async_copy(panel_source, panel, panel_sem)
    fetch.start()
    steps = width // BASE
    exact = lax.Precision.HIGHEST
    work[...] = diagonal[...]
    factor[...] = jnp.zeros_like(factor)
    inverse[...] = jnp.zeros_like(inverse)
    totals[...] = jnp.zeros_like(totals)
    row = lax.broadcasted_iota(jnp.int32, (BASE, BASE), 0)
    col = lax.broadcasted_iota(jnp.int32, (BASE, BASE), 1)

    def eliminate(step, logs):
        here = pl.ds(pl.multiple_of(step * BASE, BASE), BASE)
        upper, inverted = factor_base(work[here, here])
        factor[here, here] = jnp.where(row >= col, upper.T, 0.0)
        inverse[here, here] = inverted
        for static in range(steps):

            @pl.when(step == static)
            def _():
                start, stop = static * BASE, (static + 1) * BASE
                own = inverse[start:stop, start:stop]
                if stop < width:
                    below = dot_t(work[stop:, start:stop], own, exact)
                    factor[stop:, start:stop] = below
                    work[stop:, stop:] -= dot_t(below, below, exact)
                if start > 0:
                    product = jnp.dot(
                        factor[start:stop, :start],
                        inverse[:start, :start],
                        precision=exact,
                        preferred_element_type=jnp.float32,
                    )
                    inverse[start:stop, :start] = -jnp.dot(
                        own, product, precision=exact, preferred_element_type=jnp.float32
                    )

        pivots = jnp.sum(jnp.where(row == col, upper, 0.0), axis=0, keepdims=True)
        return logs + jnp.log(pivots)

    logs = lax.fori_loop(0, steps, eliminate, jnp.zeros((1, BASE), jnp.float32))
    store_factor = pltpu.make_async_copy(factor, factor_result, factor_sem)
    store_factor.start()
    logterm[...] = jnp.broadcast_to(2.0 * jnp.sum(logs, axis=1, keepdims=True), logterm.shape)
    high[...] = inverse[...].astype(jnp.bfloat16)
    low[...] = (inverse[...] - high[...].astype(jnp.float32)).astype(jnp.bfloat16)
    fetch.wait()
    live = counts[0]
    half = width // 2

    def solve(block, _):
        here = pl.ds(pl.multiple_of(block * width, width), width)

        @pl.when(block < live)
        def _():
            left = panel[here, :half]
            solved[here, :half] = (
                dot_t(left, high[:half, :half]) + dot_t(left, low[:half, :half])
            ).astype(jnp.bfloat16)
            left = panel[here, :]
            solved[here, half:] = (dot_t(left, high[half:, :]) + dot_t(left, low[half:, :])).astype(jnp.bfloat16)

        @pl.when(block >= live)
        def _():
            solved[here, :] = jnp.zeros((width, width), jnp.bfloat16)

        return 0

    lax.fori_loop(0, blocks, solve, 0)
    store_solved = pltpu.make_async_copy(solved, solved_result, solved_sem)
    store_solved.start()

    def update_row(i, _):
        left = pl.ds(pl.multiple_of(i * width, width), width)

        def update(j, _):
            right = pl.ds(pl.multiple_of(j * width, width), width)
            target = targets[0, i * (i + 1) // 2 + j]
            totals[target] += dot_t(solved[left, :], solved[right, :])
            return 0

        return lax.fori_loop(0, i + 1, update, 0)

    lax.fori_loop(0, live, update_row, 0)
    stores = []
    for target in range(GROUP):
        sums[target] = (-totals[target]).astype(sums.dtype)
        store = pltpu.make_async_copy(sums.at[target], sums_result.at[target], sums_sem.at[target])
        store.start()
        stores.append(store)
    for store in stores:
        store.wait()
    store_factor.wait()
    store_solved.wait()


def factor_and_update(diagonal, panel, counts, target_map):
    width = diagonal.shape[1]
    vmem = pl.BlockSpec(memory_space=pltpu.VMEM)
    smem = pl.BlockSpec(memory_space=pltpu.SMEM)
    hbm = pl.BlockSpec(memory_space=pltpu.HBM)
    return pl.pallas_call(
        factor_kernel,
        out_shape=(
            jax.ShapeDtypeStruct(diagonal.shape, jnp.float32),
            jax.ShapeDtypeStruct(panel.shape, jnp.bfloat16),
            jax.ShapeDtypeStruct((GROUP, width, width), jnp.bfloat16),
            jax.ShapeDtypeStruct((8, 128), jnp.float32),
        ),
        in_specs=[smem, smem, vmem, hbm],
        out_specs=(hbm, hbm, hbm, vmem),
        scratch_shapes=[
            pltpu.VMEM((width, width), jnp.float32),
            pltpu.VMEM((width, width), jnp.float32),
            pltpu.VMEM((width, width), jnp.bfloat16),
            pltpu.VMEM((width, width), jnp.bfloat16),
            pltpu.VMEM((GROUP, width, width), jnp.float32),
            pltpu.VMEM(diagonal.shape, jnp.float32),
            pltpu.VMEM(panel.shape, jnp.bfloat16),
            pltpu.VMEM(panel.shape, jnp.bfloat16),
            pltpu.SemaphoreType.DMA,
            pltpu.SemaphoreType.DMA,
            pltpu.SemaphoreType.DMA,
            pltpu.VMEM((GROUP, width, width), jnp.bfloat16),
            pltpu.SemaphoreType.DMA((GROUP,)),
        ],
        compiler_params=pltpu.CompilerParams(vmem_limit_bytes=60 * 1024 * 1024),
        name="factor_and_update",
    )(counts, target_map, diagonal, panel)


def exchange_kernel(
    count,
    share,
    sums,
    logterm,
    trailing,
    updated,
    logdet,
    kept,
    landed,
    partial,
    cross,
    last,
    second,
    logs,
    logs_landed,
    local_sem,
    core_send,
    core_recv,
    cross_send,
    cross_recv,
    last_send,
    last_recv,
    log_send,
    log_recv,
):
    me = lax.axis_index("dev")
    width = updated.shape[0]
    half = width // 2
    core, x, y = me % 2, me // 2 % 2, me // 4 % 2
    bits = count.bit_length() - 1

    def partner(bit):
        return me + (1 - 2 * (me // 2**bit % 2)) * 2**bit

    def remote(source, target, send, recv, bit):
        return pltpu.make_async_remote_copy(
            src_ref=source,
            dst_ref=target,
            send_sem=send,
            recv_sem=recv,
            device_id=(partner(bit),),
            device_id_type=pl.DeviceIdType.MESH,
        )

    barrier = pltpu.get_barrier_semaphore()
    for bit in range(bits):
        pl.semaphore_signal(
            barrier, inc=1, device_id=(partner(bit),), device_id_type=pl.DeviceIdType.MESH
        )
    local_copies, core_copies = [], []
    places = [(1 - y, 1 - x), (y, 1 - x), (1 - y, x), (y, x)]
    for n, (to_y, to_x) in enumerate(places):
        copy = pltpu.make_async_copy(sums.at[to_y * 4 + to_x * 2 + core], kept.at[n], local_sem.at[n])
        copy.start()
        local_copies.append(copy)
    logs[0] = logterm[...]
    pl.semaphore_wait(barrier, bits)

    order = [1, 2, 0, *range(3, bits)]
    log_copies = []

    def start_log(step):
        copy = remote(logs.at[step], logs_landed.at[step], log_send.at[step], log_recv.at[step], order[step])
        copy.start()
        log_copies.append(copy)

    def advance_log():
        step = len(log_copies) - 1
        if step < bits:
            log_copies[step].wait()
            logs[step + 1] = logs[step] + logs_landed[step]
            if step + 1 < bits:
                start_log(step + 1)
            else:
                log_copies.append(None)

    start_log(0)
    for n, (to_y, to_x) in enumerate(places):
        copy = remote(
            sums.at[to_y * 4 + to_x * 2 + 1 - core], landed.at[n], core_send.at[n], core_recv.at[n], 0
        )
        copy.start()
        core_copies.append(copy)
    upper, lower = pl.ds(0, half), pl.ds(half, half)
    x_copies = [
        remote(partial.at[n, upper], cross.at[n, upper], cross_send.at[n], cross_recv.at[n], 1)
        for n in range(2)
    ]
    y_copies = [
        remote(partial.at[2 * n, lower], cross.at[n, lower], cross_send.at[2 + n], cross_recv.at[2 + n], 2)
        for n in range(2)
    ]
    for n in range(4):
        local_copies[n].wait()
        core_copies[n].wait_recv()
        total = kept[n].astype(jnp.float32) + landed[n].astype(jnp.float32)
        if n < 3:
            partial[n] = total.astype(jnp.bfloat16)
        else:
            updated[...] = trailing[...] + total
        if n < 2:
            x_copies[n].start()
        if n == 0 or n == 2:
            y_copies[n // 2].start()
        advance_log()
    last_copies = []
    for at, own, copies, bit, n in ((upper, 2, x_copies, 2, 0), (lower, 1, y_copies, 1, 1)):
        copies[0].wait_recv()
        total = partial[own, at, :].astype(jnp.float32) + cross[0, at, :].astype(jnp.float32)
        second[at, :] = total.astype(jnp.bfloat16)
        copy = remote(second.at[at], last.at[at], last_send.at[n], last_recv.at[n], bit)
        copy.start()
        last_copies.append(copy)
    while len(log_copies) <= bits:
        advance_log()
    logdet[...] = logs[bits] * share
    for at, copies, n in ((upper, x_copies, 0), (lower, y_copies, 1)):
        copies[1].wait_recv()
        updated[at, :] += cross[1, at, :].astype(jnp.float32)
    for at, n in ((upper, 0), (lower, 1)):
        last_copies[n].wait_recv()
        updated[at, :] += last[at, :].astype(jnp.float32)
    for copy in core_copies + x_copies + y_copies + last_copies:
        copy.wait_send()


def exchange(sums, logterm, trailing):
    width = trailing.shape[1]
    count = lax.axis_size("dev")
    bits = count.bit_length() - 1
    vmem = pl.BlockSpec(memory_space=pltpu.VMEM)
    block = (width, width)
    dma = pltpu.SemaphoreType.DMA
    return pl.pallas_call(
        functools.partial(exchange_kernel, count, 1.0 / (count * width)),
        out_shape=(
            jax.ShapeDtypeStruct(trailing.shape, jnp.float32),
            jax.ShapeDtypeStruct(logterm.shape, jnp.float32),
        ),
        in_specs=[pl.BlockSpec(memory_space=pl.ANY), vmem, vmem],
        out_specs=(vmem, vmem),
        scratch_shapes=[
            pltpu.VMEM((4, *block), jnp.bfloat16),
            pltpu.VMEM((4, *block), jnp.bfloat16),
            pltpu.VMEM((3, *block), jnp.bfloat16),
            pltpu.VMEM((2, *block), jnp.bfloat16),
            pltpu.VMEM(block, jnp.bfloat16),
            pltpu.VMEM(block, jnp.bfloat16),
            pltpu.VMEM((bits + 1, *logterm.shape), jnp.float32),
            pltpu.VMEM((bits, *logterm.shape), jnp.float32),
            dma((4,)),
            dma((4,)),
            dma((4,)),
            dma((4,)),
            dma((4,)),
            dma((2,)),
            dma((2,)),
            dma((bits,)),
            dma((bits,)),
        ],
        compiler_params=pltpu.CompilerParams(
            collective_id=0, has_side_effects=True, vmem_limit_bytes=60 * 1024 * 1024
        ),
        name="exchange",
    )(sums, logterm, trailing)


def local(diagonal, panel, counts, target_map, trailing):
    factor, panel_factor, sums, logterm = factor_and_update(diagonal, panel, counts, target_map)
    updated, logdet = exchange(sums, logterm, trailing)
    return (factor, panel_factor, updated, logdet[0, 0])


def solution(mesh):
    return jax.shard_map(
        local,
        mesh=mesh,
        in_specs=(P("dev", None), P("dev", None), P("dev"), P("dev", None), P("dev", None)),
        out_specs=(P("dev", None), P("dev", None), P("dev", None), P()),
        check_vma=False,
    )
```

```python
import functools

import jax
import jax.numpy as jnp
from jax import lax
from jax.experimental import pallas as pl
from jax.experimental.pallas import tpu as pltpu
from jax.sharding import PartitionSpec as P

GROUP = 8
BASE = 128
STEP = 8
ROWS = 8
ROOM = 8


def dot_t(left, right, precision=None):
    return lax.dot_general(
        left, right, (((1,), (1,)), ((), ())), precision=precision, preferred_element_type=jnp.float32
    )


def factor_base(block):
    size = block.shape[0]
    shape = (ROWS, size)
    groups = size // ROWS
    sublane = lax.broadcasted_iota(jnp.int32, shape, 0)
    lane = lax.broadcasted_iota(jnp.int32, shape, 1)
    work = [block[g * ROWS : (g + 1) * ROWS, :] for g in range(groups)]
    side = [jnp.where(lane == sublane + g * ROWS, 1.0, 0.0).astype(jnp.float32) for g in range(groups)]
    upper, inverse = [None] * groups, [None] * groups
    for first in range(0, size, STEP):
        own, offset = first // ROWS, first % ROWS
        following = range((first + STEP) // ROWS, groups)
        columns = {
            g: [jnp.broadcast_to(work[g][:, first + j : first + j + 1], shape) for j in range(STEP)]
            for g in sorted({own, *following})
        }
        entry = {
            (i, j): jnp.broadcast_to(columns[own][j][offset + i : offset + i + 1, :], shape)
            for j in range(STEP)
            for i in range(j, STEP)
        }
        scale = []
        for j in range(STEP):
            scale.append(lax.rsqrt(entry[j, j]))
            for i in range(j + 1, STEP):
                entry[i, j] = entry[i, j] * scale[j]
            for i in range(j + 1, STEP):
                for m in range(j + 1, i + 1):
                    entry[i, m] = entry[i, m] - entry[i, j] * entry[m, j]
        rows, side_rows = [], []
        for j in range(STEP):
            row = jnp.broadcast_to(work[own][offset + j : offset + j + 1, :], shape)
            side_row = jnp.broadcast_to(side[own][offset + j : offset + j + 1, :], shape)
            for m in range(j):
                row = row - entry[j, m] * rows[m]
                side_row = side_row - entry[j, m] * side_rows[m]
            rows.append(row * scale[j])
            side_rows.append(side_row * scale[j])
        for j in range(STEP):
            at = sublane == offset + j
            upper[own] = rows[j] if upper[own] is None else jnp.where(at, rows[j], upper[own])
            inverse[own] = side_rows[j] if inverse[own] is None else jnp.where(at, side_rows[j], inverse[own])
        for g in following:
            lower = []
            for j in range(STEP):
                column = columns[g][j]
                for m in range(j):
                    column = column - lower[m] * entry[j, m]
                lower.append(column * scale[j])
            for j in range(STEP):
                work[g] = work[g] - lower[j] * rows[j]
                side[g] = side[g] - lower[j] * side_rows[j]
    return jnp.concatenate(upper, axis=0), jnp.concatenate(inverse, axis=0)


def factor_kernel(
    counts,
    targets,
    diagonal,
    panel_source,
    factor_result,
    solved_result,
    sums_result,
    logterm,
    work,
    inverse,
    high,
    low,
    totals,
    factor,
    panel,
    solved,
    panel_sem,
    factor_sem,
    solved_sem,
    sums,
    sums_sem,
):
    width = diagonal.shape[0]
    blocks = panel.shape[0] // width
    fetch = pltpu.make_async_copy(panel_source, panel, panel_sem)
    fetch.start()
    steps = width // BASE
    exact = lax.Precision.HIGHEST
    work[...] = diagonal[...]
    factor[...] = jnp.zeros_like(factor)
    inverse[...] = jnp.zeros_like(inverse)
    row = lax.broadcasted_iota(jnp.int32, (BASE, BASE), 0)
    col = lax.broadcasted_iota(jnp.int32, (BASE, BASE), 1)

    def eliminate(step, logs):
        here = pl.ds(pl.multiple_of(step * BASE, BASE), BASE)
        for extra in range(GROUP // steps):
            totals[step * (GROUP // steps) + extra] = jnp.zeros((width, width), jnp.float32)
        upper, inverted = factor_base(work[here, here])
        factor[here, here] = jnp.where(row >= col, upper.T, 0.0)
        inverse[here, here] = inverted
        for static in range(steps):

            @pl.when(step == static)
            def _():
                start, stop = static * BASE, (static + 1) * BASE
                own = inverse[start:stop, start:stop]
                if stop < width:
                    below = dot_t(work[stop:, start:stop], own, exact)
                    factor[stop:, start:stop] = below
                    work[stop:, stop:] -= dot_t(below, below, exact)
                if start > 0:
                    product = jnp.dot(
                        factor[start:stop, :start],
                        inverse[:start, :start],
                        precision=exact,
                        preferred_element_type=jnp.float32,
                    )
                    inverse[start:stop, :start] = -jnp.dot(
                        own, product, precision=exact, preferred_element_type=jnp.float32
                    )

        pivots = jnp.sum(jnp.where(row == col, upper, 0.0), axis=0, keepdims=True)
        return logs + jnp.log(pivots)

    logs = lax.fori_loop(0, steps, eliminate, jnp.zeros((1, BASE), jnp.float32))
    store_factor = pltpu.make_async_copy(factor, factor_result, factor_sem)
    store_factor.start()
    logterm[...] = jnp.broadcast_to(2.0 * jnp.sum(logs, axis=1, keepdims=True), logterm.shape)
    high[...] = inverse[...].astype(jnp.bfloat16)
    low[...] = (inverse[...] - high[...].astype(jnp.float32)).astype(jnp.bfloat16)
    fetch.wait()
    live = counts[0]
    half = width // 2

    def solve(block, _):
        here = pl.ds(pl.multiple_of(block * width, width), width)

        @pl.when(block < live)
        def _():
            left = panel[here, :half]
            solved[here, :half] = (
                dot_t(left, high[:half, :half]) + dot_t(left, low[:half, :half])
            ).astype(jnp.bfloat16)
            left = panel[here, :]
            solved[here, half:] = (dot_t(left, high[half:, :]) + dot_t(left, low[half:, :])).astype(jnp.bfloat16)

        @pl.when(block >= live)
        def _():
            solved[here, :] = jnp.zeros((width, width), jnp.bfloat16)

        return 0

    lax.fori_loop(0, blocks, solve, 0)
    store_solved = pltpu.make_async_copy(solved, solved_result, solved_sem)
    store_solved.start()

    def update(first, many):
        found = []
        for pair in [first + n for n in range(many)]:
            i = sum((pair >= r * (r + 1) // 2).astype(jnp.int32) for r in range(1, blocks))
            j = pair - i * (i + 1) // 2
            left = pl.ds(pl.multiple_of(i * width, width), width)
            right = pl.ds(pl.multiple_of(j * width, width), width)
            found.append((targets[0, pair], dot_t(solved[left, :], solved[right, :])))
        for target, product in found:
            totals[target] += product
        return 0

    pairs = live * (live + 1) // 2
    lax.fori_loop(0, pairs // 3, lambda n, _: update(3 * n, 3), 0)
    lax.fori_loop(pairs // 3 * 3, pairs, lambda n, _: update(n, 1), 0)
    stores = []
    for target in range(GROUP):
        sums[target] = (-totals[target]).astype(sums.dtype)
        store = pltpu.make_async_copy(sums.at[target], sums_result.at[target], sums_sem.at[target])
        store.start()
        stores.append(store)
    for store in stores:
        store.wait()
    store_factor.wait()
    store_solved.wait()


def factor_and_update(diagonal, panel, counts, target_map):
    width = diagonal.shape[1]
    vmem = pl.BlockSpec(memory_space=pltpu.VMEM)
    smem = pl.BlockSpec(memory_space=pltpu.SMEM)
    hbm = pl.BlockSpec(memory_space=pltpu.HBM)
    return pl.pallas_call(
        factor_kernel,
        out_shape=(
            jax.ShapeDtypeStruct(diagonal.shape, jnp.float32),
            jax.ShapeDtypeStruct(panel.shape, jnp.bfloat16),
            jax.ShapeDtypeStruct((ROOM * GROUP, width, width), jnp.bfloat16),
            jax.ShapeDtypeStruct((8, 128), jnp.float32),
        ),
        in_specs=[smem, smem, vmem, hbm],
        out_specs=(hbm, hbm, hbm, vmem),
        scratch_shapes=[
            pltpu.VMEM((width, width), jnp.float32),
            pltpu.VMEM((width, width), jnp.float32),
            pltpu.VMEM((width, width), jnp.bfloat16),
            pltpu.VMEM((width, width), jnp.bfloat16),
            pltpu.VMEM((GROUP, width, width), jnp.float32),
            pltpu.VMEM(diagonal.shape, jnp.float32),
            pltpu.VMEM(panel.shape, jnp.bfloat16),
            pltpu.VMEM(panel.shape, jnp.bfloat16),
            pltpu.SemaphoreType.DMA,
            pltpu.SemaphoreType.DMA,
            pltpu.SemaphoreType.DMA,
            pltpu.VMEM((GROUP, width, width), jnp.bfloat16),
            pltpu.SemaphoreType.DMA((GROUP,)),
        ],
        compiler_params=pltpu.CompilerParams(vmem_limit_bytes=60 * 1024 * 1024),
        name="factor_and_update",
    )(counts, target_map, diagonal, panel)


def exchange_kernel(
    count,
    share,
    sums,
    logterm,
    trailing,
    updated,
    logdet,
    kept,
    landed,
    partial,
    cross,
    last,
    second,
    logs,
    logs_landed,
    local_sem,
    core_send,
    core_recv,
    cross_send,
    cross_recv,
    last_send,
    last_recv,
    log_send,
    log_recv,
    base,
    base_sem,
):
    me = lax.axis_index("dev")
    width = updated.shape[0]
    half = width // 2
    core, x, y = me % 2, me // 2 % 2, me // 4 % 2
    bits = count.bit_length() - 1

    def partner(bit):
        return me + (1 - 2 * (me // 2**bit % 2)) * 2**bit

    def remote(source, target, send, recv, bit):
        return pltpu.make_async_remote_copy(
            src_ref=source,
            dst_ref=target,
            send_sem=send,
            recv_sem=recv,
            device_id=(partner(bit),),
            device_id_type=pl.DeviceIdType.MESH,
        )

    fetch = pltpu.make_async_copy(trailing, base, base_sem)
    fetch.start()
    barrier = pltpu.get_barrier_semaphore()
    for bit in range(bits):
        pl.semaphore_signal(
            barrier, inc=1, device_id=(partner(bit),), device_id_type=pl.DeviceIdType.MESH
        )
    local_copies, core_copies = [], []
    places = [(1 - y, 1 - x), (y, 1 - x), (1 - y, x), (y, x)]
    for n, (to_y, to_x) in enumerate(places):
        copy = pltpu.make_async_copy(sums.at[to_y * 4 + to_x * 2 + core], kept.at[n], local_sem.at[n])
        copy.start()
        local_copies.append(copy)
    logs[0] = logterm[...]
    pl.semaphore_wait(barrier, bits)

    order = [1, 2, 0, *range(3, bits)]
    log_copies = []

    def start_log(step):
        copy = remote(logs.at[step], logs_landed.at[step], log_send.at[step], log_recv.at[step], order[step])
        copy.start()
        log_copies.append(copy)

    def advance_log():
        step = len(log_copies) - 1
        if step < bits:
            log_copies[step].wait()
            logs[step + 1] = logs[step] + logs_landed[step]
            if step + 1 < bits:
                start_log(step + 1)
            else:
                log_copies.append(None)

    start_log(0)
    for n, (to_y, to_x) in enumerate(places):
        copy = remote(
            sums.at[to_y * 4 + to_x * 2 + 1 - core], landed.at[n], core_send.at[n], core_recv.at[n], 0
        )
        core_copies.append(copy)
    core_copies[0].start()
    upper, lower = pl.ds(0, half), pl.ds(half, half)
    x_copies = [
        remote(partial.at[n, upper], cross.at[n, upper], cross_send.at[n], cross_recv.at[n], 1)
        for n in range(2)
    ]
    y_copies = [
        remote(partial.at[2 * n, lower], cross.at[n, lower], cross_send.at[2 + n], cross_recv.at[2 + n], 2)
        for n in range(2)
    ]
    for n in range(4):
        local_copies[n].wait()
        core_copies[n].wait_recv()
        if n == 0:
            core_copies[1].start()
            core_copies[2].start()
        if n == 1:
            core_copies[3].start()
        total = kept[n].astype(jnp.float32) + landed[n].astype(jnp.float32)
        if n < 3:
            partial[n] = total.astype(jnp.bfloat16)
        else:
            fetch.wait()
            updated[...] = base[...] + total
        if n < 2:
            x_copies[n].start()
        if n == 0 or n == 2:
            y_copies[n // 2].start()
        advance_log()
    last_copies = []
    for at, own, copies, bit, n in ((upper, 2, x_copies, 2, 0), (lower, 1, y_copies, 1, 1)):
        copies[0].wait_recv()
        total = partial[own, at, :].astype(jnp.float32) + cross[0, at, :].astype(jnp.float32)
        second[at, :] = total.astype(jnp.bfloat16)
        copy = remote(second.at[at], last.at[at], last_send.at[n], last_recv.at[n], bit)
        copy.start()
        last_copies.append(copy)
    while len(log_copies) <= bits:
        advance_log()
    logdet[...] = logs[bits] * share
    for at, copies, n in ((upper, x_copies, 0), (lower, y_copies, 1)):
        copies[1].wait_recv()
        updated[at, :] += cross[1, at, :].astype(jnp.float32)
    for at, n in ((upper, 0), (lower, 1)):
        last_copies[n].wait_recv()
        updated[at, :] += last[at, :].astype(jnp.float32)
    for copy in core_copies + x_copies + y_copies + last_copies:
        copy.wait_send()


def exchange(sums, logterm, trailing):
    width = trailing.shape[1]
    count = lax.axis_size("dev")
    bits = count.bit_length() - 1
    vmem = pl.BlockSpec(memory_space=pltpu.VMEM)
    block = (width, width)
    dma = pltpu.SemaphoreType.DMA
    return pl.pallas_call(
        functools.partial(exchange_kernel, count, 1.0 / (count * width)),
        out_shape=(
            jax.ShapeDtypeStruct(trailing.shape, jnp.float32),
            jax.ShapeDtypeStruct(logterm.shape, jnp.float32),
        ),
        in_specs=[pl.BlockSpec(memory_space=pl.ANY), vmem, pl.BlockSpec(memory_space=pl.ANY)],
        out_specs=(vmem, vmem),
        scratch_shapes=[
            pltpu.VMEM((4, *block), jnp.bfloat16),
            pltpu.VMEM((4, *block), jnp.bfloat16),
            pltpu.VMEM((3, *block), jnp.bfloat16),
            pltpu.VMEM((2, *block), jnp.bfloat16),
            pltpu.VMEM(block, jnp.bfloat16),
            pltpu.VMEM(block, jnp.bfloat16),
            pltpu.VMEM((bits + 1, *logterm.shape), jnp.float32),
            pltpu.VMEM((bits, *logterm.shape), jnp.float32),
            dma((4,)),
            dma((4,)),
            dma((4,)),
            dma((4,)),
            dma((4,)),
            dma((2,)),
            dma((2,)),
            dma((bits,)),
            dma((bits,)),
            pltpu.VMEM(block, jnp.float32),
            dma,
        ],
        compiler_params=pltpu.CompilerParams(
            collective_id=0, has_side_effects=True, vmem_limit_bytes=32 * 1024 * 1024
        ),
        name="exchange",
    )(sums, logterm, trailing)


def local(diagonal, panel, counts, target_map, trailing):
    factor, panel_factor, sums, logterm = factor_and_update(diagonal, panel, counts, target_map)
    updated, logdet = exchange(sums, logterm, trailing)
    return (factor, panel_factor, updated, logdet[0, 0])


def solution(mesh):
    return jax.shard_map(
        local,
        mesh=mesh,
        in_specs=(P("dev", None), P("dev", None), P("dev"), P("dev", None), P("dev", None)),
        out_specs=(P("dev", None), P("dev", None), P("dev", None), P()),
        check_vma=False,
    )
```
